32 devices in a mesh: groups: 2 (over x), strip: 16 (over z, y, core).
Axes of the slice: x: 2, y: 2, z: 4, core: 2. Of those that a mesh axis runs over, the one named last changes fastest.
Arguments:
- queries: bfloat16 [32, 3, 128, 2240], P(('groups', 'strip')), parts along dimension 0, may hold values from -6 to 6
- keys: bfloat16 [32, 3, 128, 2240], P(('groups', 'strip')), parts along dimension 0, may hold values from -6 to 6
- values: bfloat16 [32, 3, 128, 2240], P(('groups', 'strip')), parts along dimension 0, may hold values from -6 to 6
- norm_gain: float32 [2240], replicated, may hold values from 0.1 to 1.9
- conv_weight: bfloat16 [3, 2240, 1152], P(None, None, 'strip'), may hold values from -0.078125 to 0.078125
Outputs:
- convolved: bfloat16 [32, 3, 128, 1152], P(('groups', 'strip')), parts along dimension 0
The draws below stay inside these ranges and needn't reach their ends.
There are 2 independent parts, one for each index of `groups`. The reference program is written for one: setup_inputs(seed, part) draws one part's arguments, and reference() takes and returns one part's arrays. A program takes and returns all parts, laid end to end along the dimension named above; an argument that names none is the same for every part. Nothing has to cross between parts.
All inputs are finite; a program needn't handle non-finite values.
Results may differ from the reference program's by a relative error of at most 0.0051.
Values may be sent and summed in bfloat16 or wider, within the bound.
A program may use at most 128 MiB of HBM per device.

```python
import jax
import jax.numpy as jnp
from jax import lax

H = 20
DH = 112
D = 2240
C_OUT = 1152
TB = 4
FB = 3
P_SIZE = 128
SLOTS = 16
N_STRIP = 16


def block_levels(key, shape, shards, smallest, top_value):
    gain = 1.0
    for position, shards_of in shards:
        draws = jax.random.uniform(jax.random.fold_in(jax.random.fold_in(key, 6), position), (shards_of,), jnp.float32, smallest / len(shards), top_value / len(shards))
        gain = gain * jnp.repeat(jnp.exp(draws), shape[position] // shards_of).reshape((-1,) + (1,) * (len(shape) - 1 - position))
    return gain


def noise(rng, extent, width, most, split=(), kind=jnp.bfloat16):
    array = width * jax.random.normal(rng, extent, jnp.float32)
    if split:
        array = array * block_levels(rng, extent, split, -0.22, 0.18)
    return jnp.clip(array, -most, most).astype(kind)


def setup_inputs(seed: int = 0, part: int = 0) -> dict:
    splits = jax.random.split(jax.random.key(seed), 6)
    own_keys = jax.random.split(jax.random.fold_in(splits[5], part), 6)
    return {
        "queries": noise(own_keys[0], (SLOTS, FB, P_SIZE, D), 1.0, 6.0, ((0, 16),)),
        "keys": noise(own_keys[1], (SLOTS, FB, P_SIZE, D), 1.0, 6.0, ((0, 16),)),
        "values": noise(own_keys[2], (SLOTS, FB, P_SIZE, D), 1.0, 6.0, ((0, 16),)),
        "norm_gain": jnp.clip(1.0 + 0.18 * jax.random.normal(splits[3], (D,), jnp.float32), 0.1, 1.9),
        "conv_weight": noise(splits[4], (3, D, C_OUT), (3 * D) ** -0.5, 0.078125, ((2, 16),)),
    }


highest = lax.Precision.HIGHEST

def reference(queries, keys, values, norm_gain, conv_weight):
    strips = N_STRIP // TB
    per_block = strips * FB * P_SIZE
    key_blocks = jax.nn.relu(keys).reshape(TB, per_block, H, DH)
    value_blocks = values.reshape(TB, per_block, H, DH)

    def block_state(pair):
        key_part, value_part = pair
        key_float = key_part.astype(jnp.float32)
        state = jnp.einsum('nhd,nhe->hde', key_float, value_part.astype(jnp.float32), precision=highest)
        return (state, lax.optimization_barrier(jnp.sum(key_float, axis=0)))
    states, sums = lax.map(block_state, (key_blocks, value_blocks))
    states = jnp.cumsum(states, axis=0)
    sums = jnp.cumsum(sums, axis=0)
    rounded = states.astype(jnp.bfloat16)
    query_blocks = jax.nn.relu(queries).reshape(TB, per_block, H, DH)

    def block_output(triple):
        query_part, state_part, sum_part = triple
        query_float = query_part.astype(jnp.float32)
        numer = jnp.einsum('nhd,hde->nhe', query_float, state_part.astype(jnp.float32), precision=highest)
        denom = jnp.einsum('nhd,hd->nh', query_float, sum_part, precision=highest) + 1e-06
        attended = (numer / denom[..., None]).reshape(per_block, H * DH)
        scale = lax.rsqrt(lax.optimization_barrier(jnp.mean(attended * attended, axis=-1, keepdims=True)) + 1e-06)
        return (attended * scale * norm_gain).astype(jnp.bfloat16)
    normed = lax.map(block_output, (query_blocks, rounded, sums))
    frames = normed.reshape(TB, strips, FB, P_SIZE, H * DH).transpose(0, 2, 1, 3, 4).reshape(TB * FB, strips * P_SIZE, H * DH)
    padded = jnp.pad(frames, ((2, 0), (0, 0), (0, 0)))

    def frame_out(index):
        total = jnp.zeros((strips * P_SIZE, C_OUT), jnp.float32)
        for tap in range(3):
            piece = lax.dynamic_index_in_dim(padded, index + 2 - tap, 0, keepdims=False)
            total = total + jnp.dot(piece, conv_weight[tap], preferred_element_type=jnp.float32)
        return total.astype(jnp.bfloat16)
    outputs = lax.map(frame_out, jnp.arange(TB * FB, dtype=jnp.int32))
    outputs = outputs.reshape(TB, FB, strips, P_SIZE, C_OUT).transpose(0, 2, 1, 3, 4)
    return outputs.reshape(N_STRIP, FB, P_SIZE, C_OUT)
```

```python
import functools

import jax
import jax.numpy as jnp
from jax import lax
from jax.experimental import pallas as pl
from jax.experimental.pallas import tpu as pltpu
from jax.sharding import PartitionSpec as P

H = 20
TB = 4
MESH = pl.DeviceIdType.MESH


def kernel(n, q_ref, k_ref, v_ref, gain_ref, w_ref, o_ref, wbuf, own, sent, got, before,
           att, x, parts, wsend, wrecv, ssend, srecv, csend, crecv, rsend, rrecv):
    frames, pixels, width = q_ref.shape
    dh = width // H
    lanes = own.shape[2]
    tokens = frames * pixels
    back = x.shape[0] - frames
    rim = back * pixels
    cols = parts.shape[2]
    strips = n // TB
    me = lax.axis_index("strip")
    block = me // strips
    bits = [1 << b for b in range(n.bit_length() - 1)]

    def across(bit):
        return me + (1 - 2 * ((me // bit) % 2)) * bit

    def owner_of(m):
        dev = me
        for bit in bits:
            dev = dev + ((m // bit) % 2) * (1 - 2 * ((me // bit) % 2)) * bit
        return dev

    ahead = (me + strips) % n
    behind = (me + n - strips) % n
    barrier = pltpu.get_barrier_semaphore()
    for dev in [across(bit) for bit in bits] + [ahead, behind]:
        pl.semaphore_signal(barrier, inc=1, device_id={"strip": dev}, device_id_type=MESH)
    wbuf[0] = w_ref[...]
    pl.semaphore_wait(barrier, len(bits) + 2)

    def weight_copy(m, bit):
        return pltpu.make_async_remote_copy(
            src_ref=wbuf.at[m], dst_ref=wbuf.at[m + bit], send_sem=wsend.at[m + bit],
            recv_sem=wrecv.at[m + bit], device_id={"strip": across(bit)}, device_id_type=MESH)

    def landing(m):
        return pltpu.make_async_remote_copy(
            src_ref=wbuf.at[m], dst_ref=wbuf.at[m], send_sem=wsend.at[m],
            recv_sem=wrecv.at[m], device_id={"strip": across(1)}, device_id_type=MESH)

    rim_copy = pltpu.make_async_remote_copy(
        src_ref=q_ref.at[pl.ds(frames - back, back)], dst_ref=x.at[pl.ds(0, back)],
        send_sem=rsend, recv_sem=rrecv, device_id={"strip": ahead}, device_id_type=MESH)
    chain_copy = pltpu.make_async_remote_copy(
        src_ref=sent, dst_ref=before, send_sem=csend, recv_sem=crecv,
        device_id={"strip": ahead}, device_id_type=MESH)

    for bit in reversed(bits):
        weight_copy(0, bit).start()

    @pl.when(block < TB - 1)
    def _():
        rim_copy.start()

    ones = jnp.ones((tokens, lanes - dh), jnp.bfloat16)
    keys = k_ref[...].reshape(tokens, width)
    values = v_ref[...].reshape(tokens, width)
    for h in range(H):
        kh = jnp.maximum(keys[:, h * dh:(h + 1) * dh], 0)
        vh = jnp.concatenate([values[:, h * dh:(h + 1) * dh], ones], axis=1)
        own[h] = lax.dot_general(kh, vh, (((0,), (0,)), ((), ())),
                                 preferred_element_type=jnp.float32)

    for s in range(strips.bit_length() - 1):
        sent[...] = own[...].astype(jnp.bfloat16)
        copy = pltpu.make_async_remote_copy(
            src_ref=sent, dst_ref=got.at[s], send_sem=ssend.at[s], recv_sem=srecv.at[s],
            device_id={"strip": across(bits[s])}, device_id_type=MESH)
        copy.start()
        copy.wait()
        own[...] = own[...] + got[s].astype(jnp.float32)

    def early(z):
        m = z * strips
        landing(m).wait_recv()
        for bit in reversed(bits):
            if bit < (m & -m):
                weight_copy(m, bit).start()

    order = sorted(range(1, TB), key=lambda z: (bin(z).count("1"), -z))
    for z in order[:2]:
        early(z)

    @pl.when(block > 0)
    def _():
        chain_copy.wait_recv()
        sent[...] = (own[...] + before[...].astype(jnp.float32)).astype(jnp.bfloat16)

    @pl.when(block == 0)
    def _():
        sent[...] = own[...].astype(jnp.bfloat16)

    @pl.when(block < TB - 1)
    def _():
        chain_copy.start()

    for z in order[2:]:
        early(z)

    def attend(queries, state, first, count):
        rows = count * pixels
        total = jnp.zeros((rows, 1), jnp.float32)
        for h in range(H):
            qh = jnp.maximum(queries[:, h * dh:(h + 1) * dh], 0)
            both = jnp.dot(qh, state[h], preferred_element_type=jnp.float32)
            a = both[:, :dh] / (both[:, dh:dh + 1] + 1e-6)
            total = total + jnp.sum(a * a, axis=1, keepdims=True)
            att[pl.ds(0, rows), h * dh:(h + 1) * dh] = a
        scale = lax.rsqrt(total / width + 1e-6)
        x[pl.ds(first, count)] = (
            att[pl.ds(0, rows), :] * scale * gain_ref[...]
        ).astype(jnp.bfloat16).reshape(count, pixels, width)

    @pl.when(block > 0)
    def _():
        rim_copy.wait_recv()
        attend(x[pl.ds(0, back)].reshape(rim, width), before, 0, back)

    @pl.when(block == 0)
    def _():
        x[pl.ds(0, back)] = jnp.zeros((back, pixels, width), jnp.bfloat16)

    attend(q_ref[...].reshape(tokens, width), sent, back, frames)

    def mix(m):
        every = lax.dot_general(
            x[...].reshape(rim + tokens, width), wbuf[m], (((1,), (1,)), ((), ())),
            preferred_element_type=jnp.float32)
        total = every[rim:, :cols]
        for j in range(1, back + 1):
            first = rim - j * pixels
            total = total + every[first:first + tokens, j * cols:(j + 1) * cols]
        parts[owner_of(m)] = total.astype(jnp.bfloat16)

    def at_hand(z, carry):
        mix(z * strips)
        return carry

    def from_core(z, carry):
        m = z * strips + 1
        landing(m).wait_recv()
        mix(m)
        return carry

    def in_pairs(i, carry):
        m = (i % TB) * strips + 2 * (1 + i // TB)
        landing(m).wait_recv()
        for bit in reversed(bits):
            if 4 * bit <= strips:
                @pl.when(m % (2 * bit) == 0)
                def _():
                    weight_copy(m, bit).start()
        mix(m)
        landing(m + 1).wait_recv()
        mix(m + 1)
        return carry

    lax.fori_loop(0, TB, at_hand, 0)
    lax.fori_loop(0, TB, from_core, 0)
    lax.fori_loop(0, TB * (strips // 2 - 1), in_pairs, 0)
    for d in range(n):
        o_ref[:, d * cols:(d + 1) * cols] = parts[d]

    def leave(m, carry):
        landing(m).wait_send()
        return carry

    lax.fori_loop(1, n, leave, 0)

    @pl.when(block < TB - 1)
    def _():
        rim_copy.wait_send()
        chain_copy.wait_send()


def per_device(queries, keys, values, norm_gain, conv_weight):
    n = lax.axis_size("strip")
    _, frames, pixels, width = queries.shape
    taps, _, cols = conv_weight.shape
    dh = width // H
    lanes = (dh + 128) // 128 * 128
    stages = max((n // TB).bit_length() - 1, 1)
    tokens = frames * pixels
    bf16, f32 = jnp.bfloat16, jnp.float32
    dma = pltpu.SemaphoreType.DMA
    out = pl.pallas_call(
        functools.partial(kernel, n),
        out_shape=jax.ShapeDtypeStruct((tokens, n * cols), bf16),
        in_specs=[pl.BlockSpec(memory_space=pltpu.VMEM)] * 5,
        out_specs=pl.BlockSpec(memory_space=pltpu.VMEM),
        scratch_shapes=[
            pltpu.VMEM((n, taps * cols, width), bf16),
            pltpu.VMEM((H, dh, lanes), f32),
            pltpu.VMEM((H, dh, lanes), bf16),
            pltpu.VMEM((stages, H, dh, lanes), bf16),
            pltpu.VMEM((H, dh, lanes), bf16),
            pltpu.VMEM((tokens, width), f32),
            pltpu.VMEM((frames + taps - 1, pixels, width), bf16),
            pltpu.VMEM((n, tokens, cols), bf16),
            dma((n,)), dma((n,)), dma((stages,)), dma((stages,)),
            dma, dma, dma, dma,
        ],
        compiler_params=pltpu.CompilerParams(
            collective_id=0, has_side_effects=True, vmem_limit_bytes=62 * 1024 * 1024),
    )(queries[0], keys[0], values[0], norm_gain[None, :], conv_weight.transpose(0, 2, 1).reshape(taps * cols, width))
    return out.reshape(1, frames, pixels, n * cols)


def solution(mesh):
    placed = (
        P(("groups", "strip"), None, None, None),
        P(("groups", "strip"), None, None, None),
        P(("groups", "strip"), None, None, None),
        P(),
        P(None, None, "strip"),
    )
    return jax.shard_map(
        per_device,
        mesh=mesh,
        in_specs=placed,
        out_specs=P(("groups", "strip"), None, None, None),
        check_vma=False,
    )
```

```python
import functools

import jax
import jax.numpy as jnp
from jax import lax
from jax.experimental import pallas as pl
from jax.experimental.pallas import tpu as pltpu
from jax.sharding import PartitionSpec as P

H = 20
TB = 4
MESH = pl.DeviceIdType.MESH


def kernel(n, q_ref, k_ref, v_ref, gain_ref, w_ref, o_ref, wbuf, own, sent, got, before,
           att, x, parts, wsend, wrecv, ssend, srecv, csend, crecv, rsend, rrecv,
           xsend):
    frames, pixels, width = q_ref.shape
    dh = width // H
    lanes = own.shape[2]
    tokens = frames * pixels
    back = x.shape[0] - frames
    rim = back * pixels
    cols = parts.shape[2]
    strips = n // TB
    me = lax.axis_index("strip")
    block = me // strips
    bits = [1 << b for b in range(n.bit_length() - 1)]

    def across(bit):
        return me + (1 - 2 * ((me // bit) % 2)) * bit

    def owner_of(m):
        dev = me
        for bit in bits:
            dev = dev + ((m // bit) % 2) * (1 - 2 * ((me // bit) % 2)) * bit
        return dev

    group = lax.axis_index("groups")
    ahead = (me + strips) % n
    behind = (me + n - strips) % n
    barrier = pltpu.get_barrier_semaphore()
    for dev in [across(bit) for bit in bits] + [ahead, behind]:
        pl.semaphore_signal(barrier, inc=1, device_id={"strip": dev}, device_id_type=MESH)
    pl.semaphore_signal(barrier, inc=1, device_id={"groups": 1 - group}, device_id_type=MESH)
    wbuf[0] = w_ref[...]
    pl.semaphore_wait(barrier, len(bits) + 3)

    def weight_copy(m, bit):
        return pltpu.make_async_remote_copy(
            src_ref=wbuf.at[m], dst_ref=wbuf.at[m + bit], send_sem=wsend.at[m + bit],
            recv_sem=wrecv.at[m + bit], device_id={"strip": across(bit)}, device_id_type=MESH)

    def twin_copy(m):
        return pltpu.make_async_remote_copy(
            src_ref=wbuf.at[m], dst_ref=wbuf.at[m], send_sem=xsend.at[m],
            recv_sem=wrecv.at[m], device_id={"groups": 1 - group}, device_id_type=MESH)

    def forward(m, limit, side):
        for bit in reversed(bits):
            if bit < limit and bit in (strips, strips // 2):
                @pl.when(group == side)
                def _():
                    weight_copy(m, bit).start()
            elif bit < limit:
                weight_copy(m, bit).start()

    def landing(m):
        return pltpu.make_async_remote_copy(
            src_ref=wbuf.at[m], dst_ref=wbuf.at[m], send_sem=wsend.at[m],
            recv_sem=wrecv.at[m], device_id={"strip": across(1)}, device_id_type=MESH)

    rim_copy = pltpu.make_async_remote_copy(
        src_ref=q_ref.at[pl.ds(frames - back, back)], dst_ref=x.at[pl.ds(0, back)],
        send_sem=rsend, recv_sem=rrecv, device_id={"strip": ahead}, device_id_type=MESH)
    chain_copy = pltpu.make_async_remote_copy(
        src_ref=sent, dst_ref=before, send_sem=csend, recv_sem=crecv,
        device_id={"strip": ahead}, device_id_type=MESH)

    forward(0, n, 0)

    @pl.when(block < TB - 1)
    def _():
        rim_copy.start()

    ones = jnp.ones((tokens, lanes - dh), jnp.bfloat16)
    keys = k_ref[...].reshape(tokens, width)
    values = v_ref[...].reshape(tokens, width)
    for h in range(H):
        kh = jnp.maximum(keys[:, h * dh:(h + 1) * dh], 0)
        vh = jnp.concatenate([values[:, h * dh:(h + 1) * dh], ones], axis=1)
        own[h] = lax.dot_general(kh, vh, (((0,), (0,)), ((), ())),
                                 preferred_element_type=jnp.float32)

    for s in range(strips.bit_length() - 1):
        sent[...] = own[...].astype(jnp.bfloat16)
        copy = pltpu.make_async_remote_copy(
            src_ref=sent, dst_ref=got.at[s], send_sem=ssend.at[s], recv_sem=srecv.at[s],
            device_id={"strip": across(bits[s])}, device_id_type=MESH)
        copy.start()
        copy.wait()
        own[...] = own[...] + got[s].astype(jnp.float32)

    far = 2 * strips
    landing(far).wait_recv()
    forward(far, far, 1)
    mine = strips + far * group
    theirs = strips + far * (1 - group)
    landing(mine).wait_recv()
    forward(mine, strips, group)
    twin_copy(mine).start()

    @pl.when(block > 0)
    def _():
        chain_copy.wait_recv()
        sent[...] = (own[...] + before[...].astype(jnp.float32)).astype(jnp.bfloat16)

    @pl.when(block == 0)
    def _():
        sent[...] = own[...].astype(jnp.bfloat16)

    @pl.when(block < TB - 1)
    def _():
        chain_copy.start()

    landing(theirs).wait_recv()
    forward(theirs, strips // 2, group)

    def attend(queries, state, first, count):
        rows = count * pixels
        total = jnp.zeros((rows, 1), jnp.float32)
        for h in range(H):
            qh = jnp.maximum(queries[:, h * dh:(h + 1) * dh], 0)
            both = jnp.dot(qh, state[h], preferred_element_type=jnp.float32)
            a = both[:, :dh] / (both[:, dh:dh + 1] + 1e-6)
            total = total + jnp.sum(a * a, axis=1, keepdims=True)
            att[pl.ds(0, rows), h * dh:(h + 1) * dh] = a
        scale = lax.rsqrt(total / width + 1e-6)
        x[pl.ds(first, count)] = (
            att[pl.ds(0, rows), :] * scale * gain_ref[...]
        ).astype(jnp.bfloat16).reshape(count, pixels, width)

    @pl.when(block > 0)
    def _():
        rim_copy.wait_recv()
        attend(x[pl.ds(0, back)].reshape(rim, width), before, 0, back)

    @pl.when(block == 0)
    def _():
        x[pl.ds(0, back)] = jnp.zeros((back, pixels, width), jnp.bfloat16)

    attend(q_ref[...].reshape(tokens, width), sent, back, frames)

    def mix(m):
        every = lax.dot_general(
            x[...].reshape(rim + tokens, width), wbuf[m], (((1,), (1,)), ((), ())),
            preferred_element_type=jnp.float32)
        total = every[rim:, :cols]
        for j in range(1, back + 1):
            first = rim - j * pixels
            total = total + every[first:first + tokens, j * cols:(j + 1) * cols]
        parts[owner_of(m)] = total.astype(jnp.bfloat16)

    def at_hand(z, carry):
        mix(z * strips)
        return carry

    def from_core(z, carry):
        m = z * strips + 1
        landing(m).wait_recv()
        mix(m)
        return carry

    def in_pairs(i, carry):
        m = ((i + group * (TB // 2)) % TB) * strips + 2 * (1 + i // TB)
        landing(m).wait_recv()

        @pl.when((m % strips == strips // 2) & ((m // far) % 2 == group))
        def _():
            twin_copy(m).start()

        for bit in reversed(bits):
            if 4 * bit <= strips:
                @pl.when(m % (2 * bit) == 0)
                def _():
                    weight_copy(m, bit).start()
        mix(m)
        landing(m + 1).wait_recv()
        mix(m + 1)
        return carry

    lax.fori_loop(0, TB, at_hand, 0)
    lax.fori_loop(0, TB, from_core, 0)
    lax.fori_loop(0, TB * (strips // 2 - 1), in_pairs, 0)
    for d in range(n):
        o_ref[:, d * cols:(d + 1) * cols] = parts[d]

    def leave(m, carry):
        shared = (m % far == strips) | (m % strips == strips // 2)
        fetched = (m // far) % 2 == group

        @pl.when(jnp.logical_not(shared) | fetched)
        def _():
            landing(m).wait_send()

        @pl.when(shared & fetched)
        def _():
            twin_copy(m).wait_send()

        return carry

    lax.fori_loop(1, n, leave, 0)

    @pl.when(block < TB - 1)
    def _():
        rim_copy.wait_send()
        chain_copy.wait_send()


def per_device(queries, keys, values, norm_gain, conv_weight):
    n = lax.axis_size("strip")
    _, frames, pixels, width = queries.shape
    taps, _, cols = conv_weight.shape
    dh = width // H
    lanes = (dh + 128) // 128 * 128
    stages = max((n // TB).bit_length() - 1, 1)
    tokens = frames * pixels
    bf16, f32 = jnp.bfloat16, jnp.float32
    dma = pltpu.SemaphoreType.DMA
    out = pl.pallas_call(
        functools.partial(kernel, n),
        out_shape=jax.ShapeDtypeStruct((tokens, n * cols), bf16),
        in_specs=[pl.BlockSpec(memory_space=pltpu.VMEM)] * 5,
        out_specs=pl.BlockSpec(memory_space=pltpu.VMEM),
        scratch_shapes=[
            pltpu.VMEM((n, taps * cols, width), bf16),
            pltpu.VMEM((H, dh, lanes), f32),
            pltpu.VMEM((H, dh, lanes), bf16),
            pltpu.VMEM((stages, H, dh, lanes), bf16),
            pltpu.VMEM((H, dh, lanes), bf16),
            pltpu.VMEM((tokens, width), f32),
            pltpu.VMEM((frames + taps - 1, pixels, width), bf16),
            pltpu.VMEM((n, tokens, cols), bf16),
            dma((n,)), dma((n,)), dma((stages,)), dma((stages,)),
            dma, dma, dma, dma, dma((n,)),
        ],
        compiler_params=pltpu.CompilerParams(
            collective_id=0, has_side_effects=True, vmem_limit_bytes=62 * 1024 * 1024),
    )(queries[0], keys[0], values[0], norm_gain[None, :], conv_weight.transpose(0, 2, 1).reshape(taps * cols, width))
    return out.reshape(1, frames, pixels, n * cols)


def solution(mesh):
    placed = (
        P(("groups", "strip"), None, None, None),
        P(("groups", "strip"), None, None, None),
        P(("groups", "strip"), None, None, None),
        P(),
        P(None, None, "strip"),
    )
    return jax.shard_map(
        per_device,
        mesh=mesh,
        in_specs=placed,
        out_specs=P(("groups", "strip"), None, None, None),
        check_vma=False,
    )
```

```python
import functools

import jax
import jax.numpy as jnp
from jax import lax
from jax.experimental import pallas as pl
from jax.experimental.pallas import tpu as pltpu
from jax.sharding import PartitionSpec as P

H = 20
TB = 4
MESH = pl.DeviceIdType.MESH


def kernel(n, q_ref, k_ref, v_ref, gain_ref, w_ref, o_ref, wbuf, own, sent, got, before,
           att, x, parts, wsend, wrecv, ssend, srecv, csend, crecv, rsend, rrecv,
           xsend):
    frames, pixels, width = q_ref.shape
    dh = width // H
    lanes = own.shape[2]
    tokens = frames * pixels
    back = x.shape[0] - frames
    rim = back * pixels
    cols = parts.shape[2]
    strips = n // TB
    me = lax.axis_index("strip")
    block = me // strips
    bits = [1 << b for b in range(n.bit_length() - 1)]

    def across(bit):
        return me + (1 - 2 * ((me // bit) % 2)) * bit

    def owner_of(m):
        dev = me
        for bit in bits:
            dev = dev + ((m // bit) % 2) * (1 - 2 * ((me // bit) % 2)) * bit
        return dev

    group = lax.axis_index("groups")
    ahead = (me + strips) % n
    behind = (me + n - strips) % n
    barrier = pltpu.get_barrier_semaphore()
    for dev in [across(bit) for bit in bits] + [ahead, behind]:
        pl.semaphore_signal(barrier, inc=1, device_id={"strip": dev}, device_id_type=MESH)
    pl.semaphore_signal(barrier, inc=1, device_id={"groups": 1 - group}, device_id_type=MESH)
    wbuf[0] = w_ref[...]
    pl.semaphore_wait(barrier, len(bits) + 3)

    def weight_copy(m, bit):
        return pltpu.make_async_remote_copy(
            src_ref=wbuf.at[m], dst_ref=wbuf.at[m + bit], send_sem=wsend.at[m + bit],
            recv_sem=wrecv.at[m + bit], device_id={"strip": across(bit)}, device_id_type=MESH)

    def twin_copy(m):
        return pltpu.make_async_remote_copy(
            src_ref=wbuf.at[m], dst_ref=wbuf.at[m], send_sem=xsend.at[m],
            recv_sem=wrecv.at[m], device_id={"groups": 1 - group}, device_id_type=MESH)

    def ours(m):
        return (m // strips) % 2 == group

    def send(m, bit):
        if bit > 1:
            weight_copy(m, bit).start()
        else:
            @pl.when(ours(m))
            def _():
                weight_copy(m, bit).start()

    def odd(m):
        landing(m).wait_recv()

        @pl.when(ours(m))
        def _():
            twin_copy(m).start()

    def landing(m):
        return pltpu.make_async_remote_copy(
            src_ref=wbuf.at[m], dst_ref=wbuf.at[m], send_sem=wsend.at[m],
            recv_sem=wrecv.at[m], device_id={"strip": across(1)}, device_id_type=MESH)

    rim_copy = pltpu.make_async_remote_copy(
        src_ref=q_ref.at[pl.ds(frames - back, back)], dst_ref=x.at[pl.ds(0, back)],
        send_sem=rsend, recv_sem=rrecv, device_id={"strip": ahead}, device_id_type=MESH)
    chain_copy = pltpu.make_async_remote_copy(
        src_ref=sent, dst_ref=before, send_sem=csend, recv_sem=crecv,
        device_id={"strip": ahead}, device_id_type=MESH)

    for bit in reversed(bits):
        send(0, bit)

    @pl.when(block < TB - 1)
    def _():
        rim_copy.start()

    ones = jnp.ones((tokens, lanes - dh), jnp.bfloat16)
    keys = k_ref[...].reshape(tokens, width)
    values = v_ref[...].reshape(tokens, width)
    for h in range(H):
        kh = jnp.maximum(keys[:, h * dh:(h + 1) * dh], 0)
        vh = jnp.concatenate([values[:, h * dh:(h + 1) * dh], ones], axis=1)
        own[h] = lax.dot_general(kh, vh, (((0,), (0,)), ((), ())),
                                 preferred_element_type=jnp.float32)

    for s in range(strips.bit_length() - 1):
        sent[...] = own[...].astype(jnp.bfloat16)
        copy = pltpu.make_async_remote_copy(
            src_ref=sent, dst_ref=got.at[s], send_sem=ssend.at[s], recv_sem=srecv.at[s],
            device_id={"strip": across(bits[s])}, device_id_type=MESH)
        copy.start()
        copy.wait()
        own[...] = own[...] + got[s].astype(jnp.float32)

    def early(z):
        m = z * strips
        landing(m).wait_recv()
        for bit in reversed(bits):
            if bit < (m & -m):
                send(m, bit)

    order = sorted(range(1, TB), key=lambda z: (bin(z).count("1"), -z))
    for z in order[:2]:
        early(z)

    @pl.when(block > 0)
    def _():
        chain_copy.wait_recv()
        sent[...] = (own[...] + before[...].astype(jnp.float32)).astype(jnp.bfloat16)

    @pl.when(block == 0)
    def _():
        sent[...] = own[...].astype(jnp.bfloat16)

    @pl.when(block < TB - 1)
    def _():
        chain_copy.start()

    for z in order[2:]:
        early(z)

    def attend(queries, state, first, count):
        rows = count * pixels
        total = jnp.zeros((rows, 1), jnp.float32)
        for h in range(H):
            qh = jnp.maximum(queries[:, h * dh:(h + 1) * dh], 0)
            both = jnp.dot(qh, state[h], preferred_element_type=jnp.float32)
            a = both[:, :dh] / (both[:, dh:dh + 1] + 1e-6)
            total = total + jnp.sum(a * a, axis=1, keepdims=True)
            att[pl.ds(0, rows), h * dh:(h + 1) * dh] = a
        scale = lax.rsqrt(total / width + 1e-6)
        x[pl.ds(first, count)] = (
            att[pl.ds(0, rows), :] * scale * gain_ref[...]
        ).astype(jnp.bfloat16).reshape(count, pixels, width)

    @pl.when(block > 0)
    def _():
        rim_copy.wait_recv()
        attend(x[pl.ds(0, back)].reshape(rim, width), before, 0, back)

    @pl.when(block == 0)
    def _():
        x[pl.ds(0, back)] = jnp.zeros((back, pixels, width), jnp.bfloat16)

    attend(q_ref[...].reshape(tokens, width), sent, back, frames)

    def mix(m):
        every = lax.dot_general(
            x[...].reshape(rim + tokens, width), wbuf[m], (((1,), (1,)), ((), ())),
            preferred_element_type=jnp.float32)
        total = every[rim:, :cols]
        for j in range(1, back + 1):
            first = rim - j * pixels
            total = total + every[first:first + tokens, j * cols:(j + 1) * cols]
        parts[owner_of(m)] = total.astype(jnp.bfloat16)

    def at_hand(z, carry):
        mix(z * strips)
        return carry

    def from_core(z, carry):
        m = z * strips + 1
        odd(m)
        mix(m)
        return carry

    def in_pairs(i, carry):
        m = (i % TB) * strips + 2 * (1 + i // TB)
        landing(m).wait_recv()
        for bit in reversed(bits):
            if 4 * bit <= strips:
                @pl.when(m % (2 * bit) == 0)
                def _():
                    send(m, bit)
        mix(m)
        odd(m + 1)
        mix(m + 1)
        return carry

    lax.fori_loop(0, TB, at_hand, 0)
    lax.fori_loop(0, TB, from_core, 0)
    lax.fori_loop(0, TB * (strips // 2 - 1), in_pairs, 0)
    for d in range(n):
        o_ref[:, d * cols:(d + 1) * cols] = parts[d]

    def leave(m, carry):
        @pl.when((m % 2 == 0) | ours(m))
        def _():
            landing(m).wait_send()

        @pl.when((m % 2 == 1) & ours(m))
        def _():
            twin_copy(m).wait_send()

        return carry

    lax.fori_loop(1, n, leave, 0)

    @pl.when(block < TB - 1)
    def _():
        rim_copy.wait_send()
        chain_copy.wait_send()


def per_device(queries, keys, values, norm_gain, conv_weight):
    n = lax.axis_size("strip")
    _, frames, pixels, width = queries.shape
    taps, _, cols = conv_weight.shape
    dh = width // H
    lanes = (dh + 128) // 128 * 128
    stages = max((n // TB).bit_length() - 1, 1)
    tokens = frames * pixels
    bf16, f32 = jnp.bfloat16, jnp.float32
    dma = pltpu.SemaphoreType.DMA
    out = pl.pallas_call(
        functools.partial(kernel, n),
        out_shape=jax.ShapeDtypeStruct((tokens, n * cols), bf16),
        in_specs=[pl.BlockSpec(memory_space=pltpu.VMEM)] * 5,
        out_specs=pl.BlockSpec(memory_space=pltpu.VMEM),
        scratch_shapes=[
            pltpu.VMEM((n, taps * cols, width), bf16),
            pltpu.VMEM((H, dh, lanes), f32),
            pltpu.VMEM((H, dh, lanes), bf16),
            pltpu.VMEM((stages, H, dh, lanes), bf16),
            pltpu.VMEM((H, dh, lanes), bf16),
            pltpu.VMEM((tokens, width), f32),
            pltpu.VMEM((frames + taps - 1, pixels, width), bf16),
            pltpu.VMEM((n, tokens, cols), bf16),
            dma((n,)), dma((n,)), dma((stages,)), dma((stages,)),
            dma, dma, dma, dma, dma((n,)),
        ],
        compiler_params=pltpu.CompilerParams(
            collective_id=0, has_side_effects=True, vmem_limit_bytes=62 * 1024 * 1024),
    )(queries[0], keys[0], values[0], norm_gain[None, :], conv_weight.transpose(0, 2, 1).reshape(taps * cols, width))
    return out.reshape(1, frames, pixels, n * cols)


def solution(mesh):
    placed = (
        P(("groups", "strip"), None, None, None),
        P(("groups", "strip"), None, None, None),
        P(("groups", "strip"), None, None, None),
        P(),
        P(None, None, "strip"),
    )
    return jax.shard_map(
        per_device,
        mesh=mesh,
        in_specs=placed,
        out_specs=P(("groups", "strip"), None, None, None),
        check_vma=False,
    )
```
